256 devices in a mesh: wide: 16 (over y, x), narrow: 16 (over z, core).
Axes of the slice: x: 4, y: 4, z: 8, core: 2. Of those that a mesh axis runs over, the one named last changes fastest.
Arguments:
- positions: float32 [3072, 3, 256], P(('wide', 'narrow')), may hold values from 6 to 18
- forces: float32 [3072, 256], P(('wide', 'narrow')), may hold values from -0.6 to 0.6
- counts: int32 [3072], P(('wide', 'narrow')), may hold values from 0 to 256, as said below
- anchors: int32 [3, 3072], P(None, ('wide', 'narrow')), may hold values from 0 to 1023, as said below
- helpers: int32 [3072, 1], P(('wide', 'narrow')), may hold values from 0 to 15, as said below
Outputs:
- spectrum: float32 [2, 128, 1024, 1024], P(None, 'wide', 'narrow')
- helper_load: float32 [16, 16], P('wide', 'narrow')
The draws below stay inside these ranges and needn't reach their ends.
Inputs may be any that keep to these rules, and one draw needn't show every extreme that they name: `counts`: within each device's 12 bins the bins with a nonzero count come first; some device has all its bins nonzero. `helpers`: within each device's 12 bins at most 1 bins name the same helper. anchors[0] < 8, anchors[1] < 64, anchors[2] < 1024.
All inputs are finite; a program needn't handle non-finite values.
Results may differ from the reference program's by a relative error of at most 0.0054.
Values may be sent and summed in bfloat16 or wider, within the bound.
No kernel may reach another device: no remote copies, remote signals or barrier semaphores. Data moves between devices by JAX's collectives and lax.ppermute only.
A program may use at most 128 MiB of HBM per device.

```python
import math
import jax
import jax.numpy as jnp
from jax import lax

XS = 8
NY = 1024
NZ = 1024
PATCH = 24
BIN = 256
BINS_DEV = 12
BINS = 3072
N_WIDE = 16
N_NARROW = 16
DEVICES = 256


def draw_positions(key, part):
    first_key, second_key, third_key = jax.random.split(key, 3)
    lowest = float(PATCH // 4)
    topmost = float(3 * PATCH // 4)
    array_dims = (BINS_DEV * DEVICES, 3, BIN)
    scattered = jax.random.uniform(first_key, array_dims, jnp.float32, lowest, topmost)
    chooser = jax.random.randint(second_key, array_dims, 0, 8)
    sided = jax.random.randint(third_key, array_dims, 0, 2)
    at_ends = jnp.where(sided == 0, jnp.float32(lowest), jnp.float32(topmost))
    end_share = 2
    return jnp.where(chooser < end_share, at_ends, scattered).astype(jnp.float32)


def draw_counts(key, part):
    first_key, second_key, third_key = jax.random.split(key, 3)
    level = jax.random.randint(first_key, (DEVICES,), 0, 8)
    living = jnp.maximum(1, BINS_DEV * level ** 3 // 343)
    filled = jax.random.randint(second_key, (), 0, DEVICES)
    living = jnp.where(jnp.arange(DEVICES) == filled, BINS_DEV, living)
    ordinal = jnp.arange(BINS_DEV)
    alive = ordinal[None, :] < living[:, None]
    sizes = jax.random.randint(third_key, (DEVICES, BINS_DEV), 1, BIN + 1)
    return jnp.where(alive, sizes, 0).reshape(-1).astype(jnp.int32)


def draw_anchors(key, part):
    limits = jnp.array([XS, NY // N_NARROW, NZ], jnp.int32)
    return jax.random.randint(key, (3, BINS_DEV * DEVICES), 0, limits[:, None]).astype(jnp.int32)


def draw_helpers(key, part):
    device_keys = jax.random.split(key, DEVICES)
    slot_total = N_NARROW * ((BINS_DEV + N_NARROW - 1) // N_NARROW)
    shuffled = jax.vmap(lambda single: jax.random.permutation(single, slot_total))(device_keys)
    chosen = shuffled[:, :BINS_DEV] // ((BINS_DEV + N_NARROW - 1) // N_NARROW)
    return chosen.reshape(BINS_DEV * DEVICES, 1).astype(jnp.int32)


def steps_of(key, dims, pieces, least, largest):
    gain, own = 1.0, jax.random.fold_in(key, 6)
    for dim, blocks in pieces:
        steps = jnp.exp(jax.random.uniform(jax.random.fold_in(own, dim), (blocks,), jnp.float32, least / len(pieces), largest / len(pieces)))
        gain = gain * jnp.repeat(steps, dims[dim] // blocks).reshape([-1 if axis == dim else 1 for axis in range(len(dims))])
    return gain


def centred(key, shape, scale, limit, pieces=(), kind=jnp.bfloat16):
    entries = jax.random.normal(key, shape, jnp.float32) * scale
    if len(pieces) > 0:
        entries = steps_of(key, shape, pieces, -0.22, 0.18) * entries
    return jnp.clip(entries, min=-limit, max=limit).astype(kind)


def setup_inputs(seed: int = 0) -> dict:
    key_list = jax.random.split(jax.random.key(seed), 6)
    positions = draw_positions(jax.random.fold_in(key_list[5], 71), 0)
    forces = centred(key_list[1], (BINS, BIN), 0.1, 0.6, ((0, 256),), jnp.float32)
    counts = draw_counts(jax.random.fold_in(key_list[5], 71), 0)
    anchors = draw_anchors(jax.random.fold_in(key_list[5], 71), 0)
    helpers = draw_helpers(jax.random.fold_in(key_list[5], 71), 0)
    return dict(positions=positions, forces=forces, counts=counts, anchors=anchors, helpers=helpers)


spread_rate = 0.08
two_pi = 2.0 * math.pi

def bin_patch(places, strength, number):
    cell_index = jnp.arange(PATCH, dtype=jnp.float32)
    living = jnp.arange(BIN, dtype=jnp.int32) < number
    weights = jnp.where(living, strength, jnp.zeros_like(strength))
    along_x = jnp.exp(-spread_rate * (cell_index[None, :] - places[0][:, None]) ** 2)
    along_y = jnp.exp(-spread_rate * (cell_index[None, :] - places[1][:, None]) ** 2)
    along_z = jnp.exp(-spread_rate * (cell_index[None, :] - places[2][:, None]) ** 2)
    left_side = weights[:, None] * along_x
    right_side = (along_y[:, :, None] * along_z[:, None, :]).reshape(BIN, PATCH * PATCH)
    return jnp.dot(left_side.T, right_side, precision=lax.Precision.HIGHEST)

def unchanged(volume):
    return volume

def dft_tables(length, columns):
    ordinal = jnp.arange(length, dtype=jnp.int32)
    phase = ordinal[:, None] * columns[None, :] % length
    angle = phase.astype(jnp.float32) * (two_pi / length)
    norm_scale = 1.0 / math.sqrt(length)
    return ((jnp.cos(angle) * norm_scale).astype(jnp.bfloat16), (jnp.sin(angle) * norm_scale).astype(jnp.bfloat16))

def reference(positions, forces, counts, anchors, helpers):
    width_x = XS * N_WIDE
    own_rows = NY // N_NARROW
    total_bins = BINS_DEV * N_WIDE * N_NARROW
    padded = jnp.zeros((width_x + PATCH, NY + PATCH, NZ + PATCH), jnp.float32)

    def place(bin_index, padded):
        bin_index = jnp.asarray(bin_index).astype(jnp.int32)
        device = bin_index // BINS_DEV
        corner = (device // N_NARROW * XS + anchors[0, bin_index], device % N_NARROW * own_rows + anchors[1, bin_index], anchors[2, bin_index])
        corner = tuple((entry.astype(jnp.int32) for entry in corner))

        def added(volume):
            patch = bin_patch(positions[bin_index], forces[bin_index], counts[bin_index])
            rounded = lax.optimization_barrier(patch.astype(jnp.bfloat16)).astype(jnp.float32)
            rounded = rounded.reshape(PATCH, PATCH, PATCH)
            region = lax.dynamic_slice(volume, corner, (PATCH, PATCH, PATCH))
            return lax.dynamic_update_slice(volume, region + rounded, corner)
        return lax.cond(counts[bin_index] > 0, added, unchanged, padded)
    padded = lax.fori_loop(0, total_bins, place, padded)
    folded = padded[:width_x].at[:PATCH].add(padded[width_x:])
    folded = folded[:, :NY].at[:, :PATCH].add(folded[:, NY:])
    folded = folded[:, :, :NZ].at[:, :, :PATCH].add(folded[:, :, NZ:])
    block_rows = NZ // N_NARROW
    slot_index = jnp.arange(NZ, dtype=jnp.int32)
    column_order = (slot_index % block_rows * N_NARROW + slot_index // block_rows).astype(jnp.int32)
    cos_z, sin_z = dft_tables(NZ, column_order)
    cos_y, sin_y = dft_tables(NY, jnp.arange(NY, dtype=jnp.int32))

    def transform(plane):
        half = plane.astype(jnp.bfloat16)
        z_real = jnp.dot(half, cos_z, preferred_element_type=jnp.float32).astype(jnp.bfloat16)
        z_imag = (-jnp.dot(half, sin_z, preferred_element_type=jnp.float32)).astype(jnp.bfloat16)
        out_real = jnp.dot(z_real.T, cos_y, preferred_element_type=jnp.float32) + jnp.dot(z_imag.T, sin_y, preferred_element_type=jnp.float32)
        out_imag = jnp.dot(z_imag.T, cos_y, preferred_element_type=jnp.float32) - jnp.dot(z_real.T, sin_y, preferred_element_type=jnp.float32)
        return jnp.stack([out_real, out_imag])
    spectra = lax.map(transform, folded)
    spectrum = jnp.moveaxis(spectra, 1, 0).astype(jnp.float32)
    group_help = helpers.reshape(N_WIDE, BINS_DEV * N_NARROW)
    group_count = counts.reshape(N_WIDE, BINS_DEV * N_NARROW).astype(jnp.float32)
    matches = group_help[:, :, None] == jnp.arange(N_NARROW, dtype=jnp.int32)[None, None, :]
    helper_load = lax.optimization_barrier(jnp.sum(jnp.where(matches, group_count[:, :, None], jnp.zeros_like(group_count)[:, :, None]), axis=1)) / BIN
    return (spectrum, helper_load.astype(jnp.float32))
```

```python
import functools
import math

import jax
import jax.numpy as jnp
import ml_dtypes
import numpy as np
from jax import lax
from jax.experimental import pallas as pl
from jax.experimental.pallas import tpu as pltpu
from jax.sharding import PartitionSpec as P

XS = 8
NY = 1024
NZ = 1024
PATCH = 24
BIN = 256
BINS_DEV = 12
SLABS = 4
CHIPS = 8
SOURCES = SLABS * CHIPS
ROWS = 56
META = 4 * BINS_DEV
RATE = 0.08
LOW = 6.0
STEP = 12.0 / 65535.0
TOP = 32767.0
TILES = 4
LANES = 128
UNROLL = 2
ENTRIES = SOURCES * BINS_DEV + UNROLL


@functools.lru_cache(maxsize=None)
def tables():
    ordinal = np.arange(NZ)
    phase = ordinal[:, None] * ordinal[None, :] % NZ
    angle = phase.astype(np.float64) * (2.0 * math.pi / NZ)
    cos = (np.cos(angle) / math.sqrt(NZ)).astype(ml_dtypes.bfloat16)
    sin = (np.sin(angle) / math.sqrt(NZ)).astype(ml_dtypes.bfloat16)
    cz = cos.reshape(NZ, 64, 16).transpose(2, 0, 1)
    sz = sin.reshape(NZ, 64, 16).transpose(2, 0, 1)
    both = np.concatenate([cz, -sz], axis=2)
    z_table = both.reshape(CHIPS, 2, NZ, LANES).transpose(0, 2, 1, 3).reshape(CHIPS, NZ, 2 * LANES)
    width = NY // TILES
    y_table = np.stack(
        [
            np.concatenate([cos[:, t * width : (t + 1) * width], sin[:, t * width : (t + 1) * width]], axis=1)
            for t in range(TILES)
        ]
    )
    return np.ascontiguousarray(z_table), np.ascontiguousarray(y_table)


def pack_kernel(counts, anchors, helpers, home, positions, forces, out):
    bins = lax.broadcasted_iota(jnp.int32, (BINS_DEV, BIN), 0)
    slot = lax.broadcasted_iota(jnp.int32, (BINS_DEV, BIN), 1)
    limit = jnp.zeros((BINS_DEV, BIN), jnp.int32)
    for b in range(BINS_DEV):
        limit = jnp.where(bins == b, counts[b], limit)
    live = jnp.where(slot < limit, forces[...], 0.0)
    largest = jnp.max(jnp.abs(live), axis=1, keepdims=True)
    power = jnp.clip(jnp.ceil(jnp.log(largest) * (1.0 / math.log(2.0))), -126.0, 1.0)
    scaled = live * jnp.exp2(-power) * TOP
    code = jnp.clip(jnp.floor(scaled + 0.5), -TOP, TOP).astype(jnp.int32)
    exponent = power.astype(jnp.int32)
    lane = lax.broadcasted_iota(jnp.int32, (1, LANES), 1)
    meta = jnp.zeros((1, LANES), jnp.int32)
    for b in range(BINS_DEV):
        place = jnp.clip((positions[b] - LOW) * (1.0 / STEP) + 0.5, 0.0, 65535.0).astype(jnp.int32)
        first = place[0:1] | (place[1:2] << 16)
        second = place[2:3] | (code[b : b + 1] << 16)
        out[4 * b : 4 * b + 1, :] = first[:, :LANES]
        out[4 * b + 1 : 4 * b + 2, :] = first[:, LANES:]
        out[4 * b + 2 : 4 * b + 3, :] = second[:, :LANES]
        out[4 * b + 3 : 4 * b + 4, :] = second[:, LANES:]
        meta = jnp.where(lane == b, counts[b], meta)
        meta = jnp.where(lane == 16 + b, home[0] * (NY // 16) + anchors[1, b], meta)
        meta = jnp.where(lane == 32 + b, anchors[0, b], meta)
        meta = jnp.where(lane == 48 + b, anchors[2, b], meta)
        meta = jnp.where(lane == 64 + b, helpers[b, 0], meta)
        meta = jnp.where(lane == 80 + b, exponent[b : b + 1, 0:1], meta)
    out[META:ROWS, :] = jnp.broadcast_to(meta, (ROWS - META, LANES))


def pack(positions, forces, counts, anchors, helpers, home):
    smem = pl.BlockSpec(memory_space=pltpu.SMEM)
    vmem = pl.BlockSpec(memory_space=pltpu.VMEM)
    return pl.pallas_call(
        pack_kernel,
        out_shape=jax.ShapeDtypeStruct((ROWS, LANES), jnp.int32),
        in_specs=[smem, smem, smem, smem, vmem, vmem],
        out_specs=vmem,
        name="pack",
    )(counts, anchors, helpers, home, positions, forces)


def spread_kernel(
    core, meta, scale, g0, g1, g2, g3, table, own, other,
    data, grid, wave, rows, offsets, ys, zs, scales,
):
    chunk = 64

    def clear(i, carry):
        at = pl.ds(pl.multiple_of(i * chunk, chunk), chunk)
        zero = jnp.zeros((chunk, LANES), jnp.float32)
        grid[0, at, :] = zero
        grid[1, at, :] = zero
        return carry

    lax.fori_loop(0, XS * (NY + PATCH) // chunk, clear, 0)
    for s, block in enumerate((g0, g1, g2, g3)):
        data[s * CHIPS * ROWS : (s + 1) * CHIPS * ROWS, :] = block[...]
    for c in range(2):
        lanes = slice(c * LANES, (c + 1) * LANES)
        wave[c, :NZ, :] = table[:, lanes].astype(jnp.float32)
        wave[c, NZ:, :] = table[:PATCH, lanes].astype(jnp.float32)

    def source(src, total):
        slab = src // CHIPS

        def more(state):
            b, _ = state
            return jnp.logical_and(b < BINS_DEV, meta[src, jnp.minimum(b, BINS_DEV - 1)] > 0)

        def add(state):
            b, k = state
            rows[k] = src * ROWS + 4 * b
            offsets[k] = XS * slab - meta[src, 32 + b]
            ys[k] = meta[src, 16 + b]
            zs[k] = meta[src, 48 + b]
            scales[k] = scale[src, b]
            return b + 1, k + 1

        return lax.while_loop(more, add, (jnp.int32(0), total))[1]

    total = lax.fori_loop(0, SOURCES, source, jnp.int32(0))
    for extra in range(UNROLL):
        rows[total + extra] = 0
        offsets[total + extra] = 0
        ys[total + extra] = 0
        zs[total + extra] = 0
        scales[total + extra] = jnp.float32(0.0)

    plane = lax.broadcasted_iota(jnp.int32, (XS, LANES), 0)
    cell = lax.broadcasted_iota(jnp.int32, (PATCH, LANES), 0).astype(jnp.float32)

    def one(k):
        row = rows[k]
        index = plane + offsets[k]
        inside = jnp.logical_and(index >= 0, index < PATCH)
        along_x = index.astype(jnp.float32)
        left, right = [], []
        for half in range(2):
            first = data[pl.ds(row + half, 1), :]
            second = data[pl.ds(row + 2 + half, 1), :]
            px = (first & 0xFFFF).astype(jnp.float32) * STEP + LOW
            py = ((first >> 16) & 0xFFFF).astype(jnp.float32) * STEP + LOW
            pz = (second & 0xFFFF).astype(jnp.float32) * STEP + LOW
            force = (second >> 16).astype(jnp.float32) * scales[k]
            ax = jnp.where(inside, jnp.exp(-RATE * (along_x - px) ** 2) * force, 0.0)
            ay = jnp.exp(-RATE * (cell - py) ** 2)
            az = jnp.exp(-RATE * (cell - pz) ** 2)
            left.append((ay[:, None, :] * ax[None, :, :]).reshape(PATCH * XS, LANES).astype(jnp.bfloat16))
            right.append(az.astype(jnp.bfloat16))
        patch = lax.dot_general(
            jnp.concatenate(left, axis=1),
            jnp.concatenate(right, axis=1),
            (((1,), (1,)), ((), ())),
            preferred_element_type=jnp.float32,
        ).astype(jnp.bfloat16)
        turn = jnp.concatenate([wave[c, pl.ds(zs[k], PATCH), :] for c in range(2)], axis=1)
        return jnp.dot(patch, turn.astype(jnp.bfloat16), preferred_element_type=jnp.float32)

    def several(i, carry):
        found = [one(UNROLL * i + u) for u in range(UNROLL)]
        for u in range(UNROLL):
            at = pl.ds(pl.multiple_of(ys[UNROLL * i + u] * XS, XS), PATCH * XS)
            grid[0, at, :] += found[u][:, :LANES]
            grid[1, at, :] += found[u][:, LANES:]
        return carry

    lax.fori_loop(0, (total + UNROLL - 1) // UNROLL, several, 0)
    grid[0, : PATCH * XS, :] += grid[0, NY * XS :, :]
    grid[1, : PATCH * XS, :] += grid[1, NY * XS :, :]
    mine = core[1]

    def finish(i, carry):
        for x in range(XS):
            at = pl.ds(i * chunk * XS + x, chunk, stride=XS)
            to = pl.ds(pl.multiple_of(i * chunk, chunk), chunk)
            own[x, to, :] = grid[mine, at, :].astype(jnp.bfloat16)
            other[x, to, :] = grid[1 - mine, at, :].astype(jnp.bfloat16)
        return carry

    lax.fori_loop(0, NY // chunk, finish, 0)


def spread(core, meta, scale, blocks, z_table):
    smem = pl.BlockSpec(memory_space=pltpu.SMEM)
    vmem = pl.BlockSpec(memory_space=pltpu.VMEM)
    half = jax.ShapeDtypeStruct((XS, NY, LANES), jnp.bfloat16)
    return pl.pallas_call(
        spread_kernel,
        out_shape=(half, half),
        grid_spec=pltpu.PrefetchScalarGridSpec(
            num_scalar_prefetch=3,
            grid=(1,),
            in_specs=[vmem] * 4 + [pl.BlockSpec((None, NZ, 2 * LANES), lambda i, core, meta, scale: (core[0], 0, 0))],
            out_specs=[vmem, vmem],
            scratch_shapes=[
                pltpu.VMEM((SOURCES * ROWS, LANES), jnp.int32),
                pltpu.VMEM((2, XS * (NY + PATCH), LANES), jnp.float32),
                pltpu.VMEM((2, NZ + PATCH, LANES), jnp.float32),
                pltpu.SMEM((ENTRIES,), jnp.int32),
                pltpu.SMEM((ENTRIES,), jnp.int32),
                pltpu.SMEM((ENTRIES,), jnp.int32),
                pltpu.SMEM((ENTRIES,), jnp.int32),
                pltpu.SMEM((ENTRIES,), jnp.float32),
            ],
        ),
        compiler_params=pltpu.CompilerParams(vmem_limit_bytes=48 * 2**20),
        name="spread",
    )(core, meta, scale, *blocks, z_table)


def rows_kernel(own, other, table, out, lines):
    @pl.when(pl.program_id(0) == 0)
    def _():
        for x in range(XS):
            both = own[x].astype(jnp.float32) + other[x].astype(jnp.float32)
            lines[x * LANES : (x + 1) * LANES, :] = both.astype(jnp.bfloat16).T

    width = NY // TILES
    waves = jnp.dot(lines[...], table[...], preferred_element_type=jnp.float32)
    for x in range(XS):
        real = waves[x * LANES : x * LANES + 64]
        imag = waves[x * LANES + 64 : (x + 1) * LANES]
        out[0, x] = real[:, :width] + imag[:, width:]
        out[1, x] = imag[:, :width] - real[:, width:]


def along_rows(own, other, y_table):
    width = NY // TILES
    vmem = pl.BlockSpec(memory_space=pltpu.VMEM)
    return pl.pallas_call(
        rows_kernel,
        out_shape=jax.ShapeDtypeStruct((2, XS, 64, NY), jnp.float32),
        grid=(TILES,),
        in_specs=[vmem, vmem, pl.BlockSpec((None, NY, 2 * width), lambda t: (t, 0, 0))],
        out_specs=pl.BlockSpec((2, XS, 64, width), lambda t: (0, 0, 0, t)),
        scratch_shapes=[pltpu.VMEM((XS * LANES, NY), jnp.bfloat16)],
        compiler_params=pltpu.CompilerParams(vmem_limit_bytes=48 * 2**20),
        name="rows",
    )(own, other, y_table)


def slab_shift(block, distance):
    count = lax.axis_size("wide")
    return lax.ppermute(block, "wide", [(i, (i + distance) % count) for i in range(count)])


def chip_shift(block, distance):
    count = lax.axis_size("narrow")
    return lax.ppermute(block, "narrow", [(i, (i + 2 * distance) % count) for i in range(count)])


def partner(block):
    count = lax.axis_size("narrow")
    return lax.ppermute(block, "narrow", [(i, i ^ 1) for i in range(count)])


def ring(block):
    near = jnp.concatenate([chip_shift(block, 1), block, chip_shift(block, -1)], axis=0)
    before = chip_shift(near, 3)
    after = chip_shift(near[: 2 * ROWS], -3)
    return jnp.concatenate([near, before, after], axis=0)


def body(positions, forces, counts, anchors, helpers):
    z_table, y_table = tables()
    home = lax.axis_index("narrow").astype(jnp.int32)
    packed = pack(positions, forces, counts, anchors, helpers, home.reshape(1))
    block = ring(packed)
    blocks = [block] + [slab_shift(block, d) for d in range(1, SLABS)]
    meta = jnp.concatenate([g.reshape(CHIPS, ROWS, LANES)[:, META] for g in blocks], axis=0)
    scale = jnp.exp2(meta[:, 80:96].astype(jnp.float32)) * (1.0 / TOP)
    numbers, choice = meta[:CHIPS, :BINS_DEV], meta[:CHIPS, 64 : 64 + BINS_DEV]
    helper_index = jnp.arange(16, dtype=jnp.int32)
    matches = choice[:, :, None] == helper_index[None, None, :]
    load = jnp.sum(jnp.where(matches, numbers[:, :, None], 0), axis=(0, 1)).astype(jnp.float32)
    load = load + partner(load)
    helper_load = (jnp.sum(jnp.where(helper_index == home, load, 0.0)) / BIN).reshape(1, 1)
    core = jnp.stack([home // 2, home % 2])
    own, other = spread(core, meta, scale, blocks, jnp.asarray(z_table))
    spectrum = along_rows(own, partner(other), jnp.asarray(y_table))
    return (spectrum, helper_load)


def solution(mesh):
    return jax.shard_map(
        body,
        mesh=mesh,
        in_specs=(
            P(("wide", "narrow"), None, None),
            P(("wide", "narrow"), None),
            P(("wide", "narrow")),
            P(None, ("wide", "narrow")),
            P(("wide", "narrow"), None),
        ),
        out_specs=(P(None, "wide", "narrow", None), P("wide", "narrow")),
        check_vma=False,
    )
```

```python
import functools
import math

import jax
import jax.numpy as jnp
import ml_dtypes
import numpy as np
from jax import lax
from jax.experimental import pallas as pl
from jax.experimental.pallas import tpu as pltpu
from jax.sharding import PartitionSpec as P

XS = 8
NY = 1024
NZ = 1024
PATCH = 24
BIN = 256
BINS_DEV = 12
SLABS = 4
CHIPS = 8
ROWS = 56
META = 4 * BINS_DEV
RATE = 0.08
LOW = 6.0
STEP = 12.0 / 65535.0
TOP = 32767.0
TILES = 4
LANES = 128
UNROLL = 16
DEPTH = NY + PATCH
WIDTH = math.sqrt(RATE * math.log2(math.e))


@functools.lru_cache(maxsize=None)
def tables():
    ordinal = np.arange(NZ)
    phase = ordinal[:, None] * ordinal[None, :] % NZ
    angle = phase.astype(np.float64) * (2.0 * math.pi / NZ)
    cos = (np.cos(angle) / math.sqrt(NZ)).astype(ml_dtypes.bfloat16)
    sin = (np.sin(angle) / math.sqrt(NZ)).astype(ml_dtypes.bfloat16)
    cz = cos.reshape(NZ, 64, 16).transpose(2, 0, 1)
    sz = sin.reshape(NZ, 64, 16).transpose(2, 0, 1)
    both = np.concatenate([cz, -sz], axis=2)
    z_table = both.reshape(CHIPS, 2, NZ, LANES).transpose(0, 2, 1, 3).reshape(CHIPS, NZ, 2 * LANES)
    width = NY // TILES
    y_table = np.stack(
        [
            np.concatenate([cos[:, t * width : (t + 1) * width], sin[:, t * width : (t + 1) * width]], axis=1)
            for t in range(TILES)
        ]
    )
    return np.ascontiguousarray(z_table), np.ascontiguousarray(y_table)


def pack_kernel(counts, anchors, helpers, home, positions, forces, out):
    bins = lax.broadcasted_iota(jnp.int32, (BINS_DEV, BIN), 0)
    slot = lax.broadcasted_iota(jnp.int32, (BINS_DEV, BIN), 1)
    limit = jnp.zeros((BINS_DEV, BIN), jnp.int32)
    for b in range(BINS_DEV):
        limit = jnp.where(bins == b, counts[b], limit)
    live = jnp.where(slot < limit, forces[...], 0.0)
    largest = jnp.max(jnp.abs(live), axis=1, keepdims=True)
    power = jnp.clip(jnp.ceil(jnp.log(largest) * (1.0 / math.log(2.0))), -126.0, 1.0)
    scaled = live * jnp.exp2(-power) * TOP
    code = jnp.clip(jnp.floor(scaled + 0.5), -TOP, TOP).astype(jnp.int32)
    exponent = power.astype(jnp.int32)
    lane = lax.broadcasted_iota(jnp.int32, (1, LANES), 1)
    meta = jnp.zeros((1, LANES), jnp.int32)
    for b in range(BINS_DEV):
        place = jnp.clip((positions[b] - LOW) * (1.0 / STEP) + 0.5, 0.0, 65535.0).astype(jnp.int32)
        first = place[0:1] | (place[1:2] << 16)
        second = place[2:3] | (code[b : b + 1] << 16)
        out[4 * b : 4 * b + 1, :] = first[:, :LANES]
        out[4 * b + 1 : 4 * b + 2, :] = first[:, LANES:]
        out[4 * b + 2 : 4 * b + 3, :] = second[:, :LANES]
        out[4 * b + 3 : 4 * b + 4, :] = second[:, LANES:]
        meta = jnp.where(lane == b, counts[b], meta)
        meta = jnp.where(lane == 16 + b, home[0] * (NY // 16) + anchors[1, b], meta)
        meta = jnp.where(lane == 32 + b, anchors[0, b], meta)
        meta = jnp.where(lane == 48 + b, anchors[2, b], meta)
        meta = jnp.where(lane == 64 + b, helpers[b], meta)
        meta = jnp.where(lane == 80 + b, exponent[b : b + 1, 0:1], meta)
    out[META:ROWS, :] = jnp.broadcast_to(meta, (ROWS - META, LANES))


def pack(positions, forces, counts, anchors, helpers, home):
    smem = pl.BlockSpec(memory_space=pltpu.SMEM)
    vmem = pl.BlockSpec(memory_space=pltpu.VMEM)
    return pl.pallas_call(
        pack_kernel,
        out_shape=jax.ShapeDtypeStruct((ROWS, LANES), jnp.int32),
        in_specs=[smem, smem, smem, smem, vmem, vmem],
        out_specs=vmem,
        name="pack",
    )(counts, anchors, helpers, home, positions, forces)


def gather_bins(meta, scale, slab, sources, lists):
    rows, offsets, ys, zs, scales = lists

    def source(src, total):
        def more(state):
            b, _ = state
            return jnp.logical_and(b < BINS_DEV, meta[src, jnp.minimum(b, BINS_DEV - 1)] > 0)

        def add(state):
            b, k = state
            rows[k] = src * ROWS + 4 * b
            offsets[k] = XS * (slab + src // CHIPS) - meta[src, 32 + b]
            ys[k] = meta[src, 16 + b]
            zs[k] = meta[src, 48 + b]
            scales[k] = scale[src, b]
            return b + 1, k + 1

        return lax.while_loop(more, add, (jnp.int32(0), total))[1]

    total = lax.fori_loop(0, sources, source, jnp.int32(0))
    for extra in range(UNROLL):
        rows[total + extra] = 0
        offsets[total + extra] = 0
        ys[total + extra] = 0
        zs[total + extra] = 0
        scales[total + extra] = jnp.float32(0.0)
    return total


def add_bins(total, lists, data, wave, grid):
    rows, offsets, ys, zs, scales = lists
    plane = lax.broadcasted_iota(jnp.int32, (XS, LANES), 0)
    cell = lax.broadcasted_iota(jnp.int32, (PATCH, LANES), 0).astype(jnp.float32) * WIDTH

    def one(k):
        row = rows[k]
        index = plane + offsets[k]
        inside = jnp.logical_and(index >= 0, index < PATCH)
        along_x = index.astype(jnp.float32) * WIDTH
        left, right = [], []
        for half in range(2):
            first = data[pl.ds(row + half, 1), :]
            second = data[pl.ds(row + 2 + half, 1), :]
            px = (first & 0xFFFF).astype(jnp.float32) * (STEP * WIDTH) + LOW * WIDTH
            py = ((first >> 16) & 0xFFFF).astype(jnp.float32) * (STEP * WIDTH) + LOW * WIDTH
            pz = (second & 0xFFFF).astype(jnp.float32) * (STEP * WIDTH) + LOW * WIDTH
            force = (second >> 16).astype(jnp.float32) * scales[k]
            dx, dy, dz = along_x - px, cell - py, cell - pz
            ax = jnp.where(inside, jnp.exp2(-(dx * dx)) * force, 0.0)
            ay = jnp.exp2(-(dy * dy))
            az = jnp.exp2(-(dz * dz))
            products = [ay * ax[x : x + 1, :] for x in range(XS)]
            left.append(jnp.concatenate(products, axis=0).astype(jnp.bfloat16))
            right.append(az.astype(jnp.bfloat16))
        patch = lax.dot_general(
            jnp.concatenate(left, axis=1),
            jnp.concatenate(right, axis=1),
            (((1,), (1,)), ((), ())),
            preferred_element_type=jnp.float32,
        ).astype(jnp.bfloat16)
        turn = jnp.concatenate([wave[c, pl.ds(zs[k], PATCH), :] for c in range(2)], axis=1)
        return jnp.dot(patch, turn.astype(jnp.bfloat16), preferred_element_type=jnp.float32)

    def several(i, carry):
        found = [one(UNROLL * i + u) for u in range(UNROLL)]
        for u in range(UNROLL):
            y = ys[UNROLL * i + u]
            for c in range(2):
                for x in range(XS):
                    at = pl.ds((c * XS + x) * DEPTH + y, PATCH)
                    grid[at, :] += found[u][x * PATCH : (x + 1) * PATCH, c * LANES : (c + 1) * LANES]
        return carry

    lax.fori_loop(0, (total + UNROLL - 1) // UNROLL, several, 0)

def near_kernel(chip, meta, scale, block, table, grid, wave, *lists):
    def clear(i, carry):
        at = pl.ds(pl.multiple_of(i * DEPTH, XS), DEPTH)
        grid[at, :] = jnp.zeros((DEPTH, LANES), jnp.float32)
        return carry

    lax.fori_loop(0, 2 * XS, clear, 0)
    for c in range(2):
        lanes = slice(c * LANES, (c + 1) * LANES)
        wave[c, :NZ, :] = table[:, lanes].astype(jnp.float32)
        wave[c, NZ:, :] = table[:PATCH, lanes].astype(jnp.float32)
    total = gather_bins(meta, scale, 0, CHIPS, lists)
    add_bins(total, lists, block, wave, grid)


def far_kernel(core, meta, scale, g1, g2, g3, wave, grid_in, own, other, grid, data, *lists):
    for s, block in enumerate((g1, g2, g3)):
        data[s * CHIPS * ROWS : (s + 1) * CHIPS * ROWS, :] = block[...]
    total = gather_bins(meta, scale, 1, (SLABS - 1) * CHIPS, lists)
    add_bins(total, lists, data, wave, grid)
    mine = core[0]

    def finish(i, carry):
        for c, half in ((mine, own), (1 - mine, other)):
            start = pl.multiple_of((c * XS + i) * DEPTH, XS)
            grid[pl.ds(start, PATCH), :] += grid[pl.ds(start + NY, PATCH), :]
            half[i] = grid[pl.ds(start, NY), :].astype(jnp.bfloat16)
        return carry

    lax.fori_loop(0, XS, finish, 0)


def bin_lists(sources):
    entries = sources * BINS_DEV + UNROLL
    return [pltpu.SMEM((entries,), jnp.int32)] * 4 + [pltpu.SMEM((entries,), jnp.float32)]


def spread_near(chip, meta, scale, block, z_table):
    smem = pl.BlockSpec(memory_space=pltpu.SMEM)
    vmem = pl.BlockSpec(memory_space=pltpu.VMEM)
    return pl.pallas_call(
        near_kernel,
        out_shape=(
            pltpu.VMEM((2 * XS * DEPTH, LANES), jnp.float32),
            pltpu.VMEM((2, DEPTH, LANES), jnp.float32),
        ),
        grid_spec=pltpu.PrefetchScalarGridSpec(
            num_scalar_prefetch=3,
            grid=(1,),
            in_specs=[vmem, pl.BlockSpec((None, NZ, 2 * LANES), lambda i, chip, meta, scale: (chip[0], 0, 0))],
            out_specs=[vmem, vmem],
            scratch_shapes=bin_lists(CHIPS),
        ),
        compiler_params=pltpu.CompilerParams(vmem_limit_bytes=24 * 2**20),
        cost_estimate=pl.CostEstimate(flops=2**32, bytes_accessed=2**23, transcendentals=2**20),
        name="near",
    )(chip, meta, scale, block, z_table)


def spread_far(core, meta, scale, blocks, wave, grid):
    smem = pl.BlockSpec(memory_space=pltpu.SMEM)
    vmem = pl.BlockSpec(memory_space=pltpu.VMEM)
    half = (XS, NY, LANES)
    sources = (SLABS - 1) * CHIPS
    return pl.pallas_call(
        far_kernel,
        out_shape=(
            pltpu.VMEM(half, jnp.bfloat16),
            jax.ShapeDtypeStruct(half, jnp.bfloat16),
            pltpu.VMEM((2 * XS * DEPTH, LANES), jnp.float32),
        ),
        in_specs=[smem] * 3 + [vmem] * 5,
        out_specs=[vmem] * 3,
        input_output_aliases={7: 2},
        scratch_shapes=[pltpu.VMEM((sources * ROWS, LANES), jnp.int32)] + bin_lists(sources),
        compiler_params=pltpu.CompilerParams(vmem_limit_bytes=24 * 2**20),
        name="far",
    )(core, meta, scale, *blocks, wave, grid)


def rows_kernel(own, other, table, out, lines):
    @pl.when(pl.program_id(0) == 0)
    def _():
        for x in range(XS):
            both = own[x].astype(jnp.float32) + other[x].astype(jnp.float32)
            lines[x * LANES : (x + 1) * LANES, :] = both.astype(jnp.bfloat16).T

    width = NY // TILES
    waves = jnp.dot(lines[...], table[...], preferred_element_type=jnp.float32)
    for x in range(XS):
        real = waves[x * LANES : x * LANES + 64]
        imag = waves[x * LANES + 64 : (x + 1) * LANES]
        out[0, x] = real[:, :width] + imag[:, width:]
        out[1, x] = imag[:, :width] - real[:, width:]


def along_rows(own, other, y_table):
    width = NY // TILES
    vmem = pl.BlockSpec(memory_space=pltpu.VMEM)
    return pl.pallas_call(
        rows_kernel,
        out_shape=jax.ShapeDtypeStruct((2, XS, 64, NY), jnp.float32),
        grid=(TILES,),
        in_specs=[vmem, vmem, pl.BlockSpec((None, NY, 2 * width), lambda t: (t, 0, 0))],
        out_specs=pl.BlockSpec((2, XS, 64, width), lambda t: (0, 0, 0, t)),
        scratch_shapes=[pltpu.VMEM((XS * LANES, NY), jnp.bfloat16)],
        compiler_params=pltpu.CompilerParams(vmem_limit_bytes=48 * 2**20),
        name="rows",
    )(own, other, y_table)


def slab_shift(block, distance):
    count = lax.axis_size("wide")
    return lax.ppermute(block, "wide", [(i, (i + distance) % count) for i in range(count)])


def chip_shift(block, distance):
    count = lax.axis_size("narrow")
    return lax.ppermute(block, "narrow", [(i, (i + 2 * distance) % count) for i in range(count)])


def partner(block):
    count = lax.axis_size("narrow")
    return lax.ppermute(block, "narrow", [(i, i ^ 1) for i in range(count)])


def ring(block):
    near = jnp.concatenate([chip_shift(block, 1), block, chip_shift(block, -1)], axis=0)
    before = chip_shift(near, 3)
    after = chip_shift(near[: 2 * ROWS], -3)
    return jnp.concatenate([near, before, after], axis=0)


def powers(meta):
    return jnp.exp2(meta[:, 80:96].astype(jnp.float32)) * (1.0 / TOP)


def body(positions, forces, counts, anchors, helpers):
    z_table, y_table = tables()
    home = lax.axis_index("narrow").astype(jnp.int32)
    packed = pack(positions, forces, counts, anchors, helpers.reshape(BINS_DEV), home.reshape(1))
    block = ring(packed)
    blocks = [slab_shift(block, d) for d in range(1, SLABS)]
    here = block.reshape(CHIPS, ROWS, LANES)[:, META]
    numbers, choice = here[:, :BINS_DEV], here[:, 64 : 64 + BINS_DEV]
    helper_index = jnp.arange(16, dtype=jnp.int32)
    matches = choice[:, :, None] == helper_index[None, None, :]
    load = jnp.sum(jnp.where(matches, numbers[:, :, None], 0), axis=(0, 1)).astype(jnp.float32)
    load = load + partner(load)
    grid, wave = spread_near((home // 2).reshape(1), here, powers(here), block, pltpu.with_memory_space_constraint(jnp.asarray(z_table), pltpu.HBM))
    wave, load = lax.optimization_barrier((wave, load))
    helper_load = (jnp.sum(jnp.where(helper_index == home, load, 0.0)) / BIN).reshape(1, 1)
    meta = jnp.concatenate([g.reshape(CHIPS, ROWS, LANES)[:, META] for g in blocks], axis=0)
    own, other, _ = spread_far((home % 2).reshape(1), meta, powers(meta), blocks, wave, grid)
    spectrum = along_rows(own, partner(other), jnp.asarray(y_table))
    return (spectrum, helper_load)


def solution(mesh):
    return jax.shard_map(
        body,
        mesh=mesh,
        in_specs=(
            P(("wide", "narrow"), None, None),
            P(("wide", "narrow"), None),
            P(("wide", "narrow")),
            P(None, ("wide", "narrow")),
            P(("wide", "narrow"), None),
        ),
        out_specs=(P(None, "wide", "narrow", None), P("wide", "narrow")),
        check_vma=False,
    )
```

```python
import functools
import math

import jax
import jax.numpy as jnp
import ml_dtypes
import numpy as np
from jax import lax
from jax.experimental import pallas as pl
from jax.experimental.pallas import tpu as pltpu
from jax.sharding import PartitionSpec as P

XS = 8
NY = 1024
NZ = 1024
PATCH = 24
BIN = 256
BINS_DEV = 12
SLABS = 4
CHIPS = 8
ROWS = 56
META = 4 * BINS_DEV
RATE = 0.08
LOW = 6.0
STEP = 12.0 / 65535.0
TOP = 32767.0
TILES = 1
PLANES = 2
LANES = 128
UNROLL = 16
DEPTH = NY + PATCH
WIDTH = math.sqrt(RATE * math.log2(math.e))


@functools.lru_cache(maxsize=None)
def tables():
    ordinal = np.arange(NZ)
    phase = ordinal[:, None] * ordinal[None, :] % NZ
    angle = phase.astype(np.float64) * (2.0 * math.pi / NZ)
    cos = (np.cos(angle) / math.sqrt(NZ)).astype(ml_dtypes.bfloat16)
    sin = (np.sin(angle) / math.sqrt(NZ)).astype(ml_dtypes.bfloat16)
    cz = cos.reshape(NZ, 64, 16).transpose(2, 0, 1)
    sz = sin.reshape(NZ, 64, 16).transpose(2, 0, 1)
    both = np.concatenate([cz, -sz], axis=2)
    z_table = both.reshape(CHIPS, 2, NZ, LANES).transpose(0, 2, 1, 3).reshape(CHIPS, NZ, 2 * LANES)
    y_table = np.stack([cos, sin])
    return np.ascontiguousarray(z_table), np.ascontiguousarray(y_table)


def pack_kernel(counts, anchors, helpers, home, positions, forces, out):
    bins = lax.broadcasted_iota(jnp.int32, (BINS_DEV, BIN), 0)
    slot = lax.broadcasted_iota(jnp.int32, (BINS_DEV, BIN), 1)
    limit = jnp.zeros((BINS_DEV, BIN), jnp.int32)
    for b in range(BINS_DEV):
        limit = jnp.where(bins == b, counts[b], limit)
    live = jnp.where(slot < limit, forces[...], 0.0)
    largest = jnp.max(jnp.abs(live), axis=1, keepdims=True)
    power = jnp.clip(jnp.ceil(jnp.log(largest) * (1.0 / math.log(2.0))), -126.0, 1.0)
    scaled = live * jnp.exp2(-power) * TOP
    code = jnp.clip(jnp.floor(scaled + 0.5), -TOP, TOP).astype(jnp.int32)
    exponent = power.astype(jnp.int32)
    lane = lax.broadcasted_iota(jnp.int32, (1, LANES), 1)
    meta = jnp.zeros((1, LANES), jnp.int32)
    for b in range(BINS_DEV):
        place = jnp.clip((positions[b] - LOW) * (1.0 / STEP) + 0.5, 0.0, 65535.0).astype(jnp.int32)
        first = place[0:1] | (place[1:2] << 16)
        second = place[2:3] | (code[b : b + 1] << 16)
        out[4 * b : 4 * b + 1, :] = first[:, :LANES]
        out[4 * b + 1 : 4 * b + 2, :] = first[:, LANES:]
        out[4 * b + 2 : 4 * b + 3, :] = second[:, :LANES]
        out[4 * b + 3 : 4 * b + 4, :] = second[:, LANES:]
        meta = jnp.where(lane == b, counts[b], meta)
        meta = jnp.where(lane == 16 + b, home[0] * (NY // 16) + anchors[1, b], meta)
        meta = jnp.where(lane == 32 + b, anchors[0, b], meta)
        meta = jnp.where(lane == 48 + b, anchors[2, b], meta)
        meta = jnp.where(lane == 64 + b, helpers[b], meta)
        meta = jnp.where(lane == 80 + b, exponent[b : b + 1, 0:1], meta)
    out[META:ROWS, :] = jnp.broadcast_to(meta, (ROWS - META, LANES))


def pack(positions, forces, counts, anchors, helpers, home):
    smem = pl.BlockSpec(memory_space=pltpu.SMEM)
    vmem = pl.BlockSpec(memory_space=pltpu.VMEM)
    return pl.pallas_call(
        pack_kernel,
        out_shape=jax.ShapeDtypeStruct((ROWS, LANES), jnp.int32),
        in_specs=[smem, smem, smem, smem, vmem, vmem],
        out_specs=vmem,
        name="pack",
    )(counts, anchors, helpers, home, positions, forces)


def gather_bins(metas, slab, lists):
    rows, offsets, ys, zs, powers = lists
    total = jnp.int32(0)
    for s, meta in enumerate(metas):

        def source(src, total, meta=meta, s=s):
            def more(state):
                b, _ = state
                return jnp.logical_and(b < BINS_DEV, meta[src, jnp.minimum(b, BINS_DEV - 1)] > 0)

            def add(state):
                b, k = state
                rows[k] = (s * CHIPS + src) * ROWS + 4 * b
                offsets[k] = XS * (slab + s) - meta[src, 32 + b]
                ys[k] = meta[src, 16 + b]
                zs[k] = meta[src, 48 + b]
                powers[k] = meta[src, 80 + b]
                return b + 1, k + 1

            return lax.while_loop(more, add, (jnp.int32(0), total))[1]

        total = lax.fori_loop(0, CHIPS, source, total)
    for extra in range(UNROLL):
        rows[total + extra] = 0
        offsets[total + extra] = 0
        ys[total + extra] = 0
        zs[total + extra] = 0
        powers[total + extra] = -1000
    return total


def add_bins(total, lists, data, wave, grid):
    rows, offsets, ys, zs, powers = lists
    plane = lax.broadcasted_iota(jnp.int32, (XS, LANES), 0)
    cell = lax.broadcasted_iota(jnp.int32, (PATCH, LANES), 0).astype(jnp.float32) * WIDTH

    def one(k):
        row = rows[k]
        index = plane + offsets[k]
        inside = jnp.logical_and(index >= 0, index < PATCH)
        along_x = index.astype(jnp.float32) * WIDTH
        scale = jnp.exp2(jnp.full((1, LANES), powers[k], jnp.int32).astype(jnp.float32)) * (1.0 / TOP)
        left, right = [], []
        for half in range(2):
            first = data[pl.ds(row + half, 1), :]
            second = data[pl.ds(row + 2 + half, 1), :]
            px = (first & 0xFFFF).astype(jnp.float32) * (STEP * WIDTH) + LOW * WIDTH
            py = ((first >> 16) & 0xFFFF).astype(jnp.float32) * (STEP * WIDTH) + LOW * WIDTH
            pz = (second & 0xFFFF).astype(jnp.float32) * (STEP * WIDTH) + LOW * WIDTH
            force = (second >> 16).astype(jnp.float32) * scale
            dx, dy, dz = along_x - px, cell - py, cell - pz
            ax = jnp.where(inside, jnp.exp2(-(dx * dx)) * force, 0.0)
            ay = jnp.exp2(-(dy * dy))
            az = jnp.exp2(-(dz * dz))
            products = [ay * ax[x : x + 1, :] for x in range(XS)]
            left.append(jnp.concatenate(products, axis=0).astype(jnp.bfloat16))
            right.append(az.astype(jnp.bfloat16))
        patch = lax.dot_general(
            jnp.concatenate(left, axis=1),
            jnp.concatenate(right, axis=1),
            (((1,), (1,)), ((), ())),
            preferred_element_type=jnp.float32,
        ).astype(jnp.bfloat16)
        turn = jnp.concatenate([wave[c, pl.ds(zs[k], PATCH), :] for c in range(2)], axis=1)
        return jnp.dot(patch, turn.astype(jnp.bfloat16), preferred_element_type=jnp.float32)

    def several(i, carry):
        found = [one(UNROLL * i + u) for u in range(UNROLL)]
        for u in range(UNROLL):
            y = ys[UNROLL * i + u]
            for c in range(2):
                for x in range(XS):
                    at = pl.ds((c * XS + x) * DEPTH + y, PATCH)
                    grid[at, :] += found[u][x * PATCH : (x + 1) * PATCH, c * LANES : (c + 1) * LANES]
        return carry

    lax.fori_loop(0, (total + UNROLL - 1) // UNROLL, several, 0)

def near_kernel(chip, meta, block, table, grid, wave, load, *lists):
    def clear(i, carry):
        at = pl.ds(pl.multiple_of(i * DEPTH, XS), DEPTH)
        grid[at, :] = jnp.zeros((DEPTH, LANES), jnp.float32)
        return carry

    lax.fori_loop(0, 2 * XS, clear, 0)
    for c in range(2):
        lanes = slice(c * LANES, (c + 1) * LANES)
        wave[c, :NZ, :] = table[:, lanes].astype(jnp.float32)
        wave[c, NZ:, :] = table[:PATCH, lanes].astype(jnp.float32)
    lane = lax.broadcasted_iota(jnp.int32, (1, LANES), 1)
    count = jnp.zeros((1, LANES), jnp.int32)
    for src in range(CHIPS):
        row = block[src * ROWS + META : src * ROWS + META + 1, :]
        for b in range(BINS_DEV):
            count += jnp.where(lane == row[:, 64 + b : 65 + b], row[:, b : b + 1], 0)
    load[...] = jnp.broadcast_to(count, (8, LANES))
    total = gather_bins((meta,), 0, lists)
    add_bins(total, lists, block, wave, grid)


def far_kernel(core, m1, m2, m3, g1, g2, g3, wave, load, grid_in, own, other, grid, data, *lists):
    for s, block in enumerate((g1, g2, g3)):
        data[s * CHIPS * ROWS : (s + 1) * CHIPS * ROWS, :] = block[...]
    total = gather_bins((m1, m2, m3), 1, lists)
    add_bins(total, lists, data, wave, grid)
    mine = core[0]

    def finish(i, carry):
        for c, half in ((mine, own), (1 - mine, other)):
            start = pl.multiple_of((c * XS + i) * DEPTH, XS)
            grid[pl.ds(start, PATCH), :] += grid[pl.ds(start + NY, PATCH), :]
            half[pl.ds(pl.multiple_of(i * NY, NY), NY), :] = grid[pl.ds(start, NY), :].astype(jnp.bfloat16)
        return carry

    lax.fori_loop(0, XS, finish, 0)
    row = lax.broadcasted_iota(jnp.int32, (16, LANES), 0)
    count = jnp.concatenate([load[...], load[...]], axis=0)
    tail = jnp.where(row == 0, count >> 8, jnp.where(row == 1, count & 255, 0))
    other[XS * NY :, :] = tail.astype(jnp.float32).astype(jnp.bfloat16)


def bin_lists(slabs):
    return [pltpu.SMEM((slabs * CHIPS * BINS_DEV + UNROLL,), jnp.int32)] * 5


def spread_near(chip, meta, block, z_table):
    vmem = pl.BlockSpec(memory_space=pltpu.VMEM)
    return pl.pallas_call(
        near_kernel,
        out_shape=(
            pltpu.VMEM((2 * XS * DEPTH, LANES), jnp.float32),
            pltpu.VMEM((2, DEPTH, LANES), jnp.float32),
            pltpu.VMEM((8, LANES), jnp.int32),
        ),
        grid_spec=pltpu.PrefetchScalarGridSpec(
            num_scalar_prefetch=2,
            grid=(1,),
            in_specs=[vmem, pl.BlockSpec((None, NZ, 2 * LANES), lambda i, chip, meta: (chip[0], 0, 0))],
            out_specs=[vmem, vmem, vmem],
            scratch_shapes=bin_lists(1),
        ),
        compiler_params=pltpu.CompilerParams(vmem_limit_bytes=24 * 2**20),
        cost_estimate=pl.CostEstimate(flops=2**32, bytes_accessed=2**23, transcendentals=2**20),
        name="near",
    )(chip, meta, block, z_table)


def spread_far(core, metas, blocks, wave, load, grid):
    smem = pl.BlockSpec(memory_space=pltpu.SMEM)
    vmem = pl.BlockSpec(memory_space=pltpu.VMEM)
    return pl.pallas_call(
        far_kernel,
        out_shape=(
            pltpu.VMEM((XS * NY, LANES), jnp.bfloat16),
            pltpu.VMEM((XS * NY + 16, LANES), jnp.bfloat16),
            pltpu.VMEM((2 * XS * DEPTH, LANES), jnp.float32),
        ),
        in_specs=[smem] * 4 + [vmem] * 6,
        out_specs=[vmem] * 3,
        input_output_aliases={9: 2},
        scratch_shapes=[pltpu.VMEM(((SLABS - 1) * CHIPS * ROWS, LANES), jnp.int32)] + bin_lists(SLABS - 1),
        compiler_params=pltpu.CompilerParams(vmem_limit_bytes=24 * 2**20),
        name="far",
    )(core, *metas, *blocks, wave, load, grid)


def rows_kernel(home, own, other, load, table, out, helper_load):
    step = pl.program_id(0)

    @pl.when(step == 0)
    def _():
        theirs = other[XS * NY :, :].astype(jnp.float32)
        both = load[0:1, :].astype(jnp.float32) + theirs[0:1] * 256.0 + theirs[1:2]
        lane = lax.broadcasted_iota(jnp.int32, (1, LANES), 1)
        helper_load[0, 0] = jnp.sum(jnp.where(lane == home[0], both, 0.0)) * (1.0 / BIN)

    lines = []
    for x in range(PLANES):
        at = pl.ds(pl.multiple_of((step * PLANES + x) * NY, NY), NY)
        both = own[at, :].astype(jnp.float32) + other[at, :].astype(jnp.float32)
        lines.append(both.astype(jnp.bfloat16).T)
    lines = jnp.concatenate(lines, axis=0)
    width = NY // TILES
    for t in range(TILES):
        at = slice(t * width, (t + 1) * width)
        cos = jnp.dot(lines, table[0, :, at], preferred_element_type=jnp.float32)
        sin = jnp.dot(lines, table[1, :, at], preferred_element_type=jnp.float32)
        for x in range(PLANES):
            real = slice(x * LANES, x * LANES + 64)
            imag = slice(x * LANES + 64, (x + 1) * LANES)
            out[0, x, :, at] = cos[real] + sin[imag]
            out[1, x, :, at] = cos[imag] - sin[real]


def along_rows(home, own, other, load, y_table):
    smem = pl.BlockSpec(memory_space=pltpu.SMEM)
    vmem = pl.BlockSpec(memory_space=pltpu.VMEM)
    return pl.pallas_call(
        rows_kernel,
        out_shape=(
            jax.ShapeDtypeStruct((2, XS, 64, NY), jnp.float32),
            jax.ShapeDtypeStruct((1, 1), jnp.float32),
        ),
        grid=(XS // PLANES,),
        in_specs=[
            smem,
            vmem,
            vmem,
            vmem,
            vmem,
        ],
        out_specs=[pl.BlockSpec((2, PLANES, 64, NY), lambda i: (0, i, 0, 0)), smem],
        compiler_params=pltpu.CompilerParams(vmem_limit_bytes=24 * 2**20),
        name="rows",
    )(home, own, other, load, y_table)


def slab_shift(block, distance):
    count = lax.axis_size("wide")
    return lax.ppermute(block, "wide", [(i, (i + distance) % count) for i in range(count)])


def chip_shift(block, distance):
    count = lax.axis_size("narrow")
    return lax.ppermute(block, "narrow", [(i, (i + 2 * distance) % count) for i in range(count)])


def partner(block):
    count = lax.axis_size("narrow")
    return lax.ppermute(block, "narrow", [(i, i ^ 1) for i in range(count)])


def ring(block):
    near = jnp.concatenate([chip_shift(block, 1), block, chip_shift(block, -1)], axis=0)
    before = chip_shift(near, 3)
    after = chip_shift(near[: 2 * ROWS], -3)
    return jnp.concatenate([near, before, after], axis=0)


def metas_of(block):
    return block.reshape(CHIPS, ROWS, LANES)[:, META]


def body(positions, forces, counts, anchors, helpers):
    z_table, y_table = tables()
    z_table = pltpu.with_memory_space_constraint(jnp.asarray(z_table), pltpu.HBM)
    y_table = pltpu.with_memory_space_constraint(jnp.asarray(y_table), pltpu.VMEM)
    index = lax.axis_index("narrow").astype(jnp.int32)
    home, chip, core = index.reshape(1), (index >> 1).reshape(1), (index & 1).reshape(1)
    packed = pack(positions, forces, counts, anchors, helpers.reshape(BINS_DEV), home)
    block = ring(packed)
    blocks = [slab_shift(block, d) for d in range(1, SLABS)]
    grid, wave, load = spread_near(chip, metas_of(block), block, z_table)
    own, other, _ = spread_far(core, [metas_of(g) for g in blocks], blocks, wave, load, grid)
    arrived = pltpu.with_memory_space_constraint(partner(other), pltpu.VMEM)
    spectrum, helper_load = along_rows(home, own, arrived, load, y_table)
    return (spectrum, helper_load)


def solution(mesh):
    return jax.shard_map(
        body,
        mesh=mesh,
        in_specs=(
            P(("wide", "narrow"), None, None),
            P(("wide", "narrow"), None),
            P(("wide", "narrow")),
            P(None, ("wide", "narrow")),
            P(("wide", "narrow"), None),
        ),
        out_specs=(P(None, "wide", "narrow", None), P("wide", "narrow")),
        check_vma=False,
    )
```

```python
import functools
import math

import jax
import jax.numpy as jnp
import ml_dtypes
import numpy as np
from jax import lax
from jax.experimental import pallas as pl
from jax.experimental.pallas import tpu as pltpu
from jax.sharding import PartitionSpec as P

XS = 8
NY = 1024
NZ = 1024
PATCH = 24
BIN = 256
BINS_DEV = 12
SLABS = 4
CHIPS = 8
ROWS = 56
META = 4 * BINS_DEV
RATE = 0.08
LOW = 6.0
STEP = 12.0 / 65535.0
TOP = 32767.0
TILES = 4
PLANES = 4
LANES = 128
NEAR = 16
FAR = 24
DEPTH = NY + PATCH
WIDTH = math.sqrt(RATE * math.log2(math.e))


@functools.lru_cache(maxsize=None)
def tables():
    ordinal = np.arange(NZ)
    phase = ordinal[:, None] * ordinal[None, :] % NZ
    angle = phase.astype(np.float64) * (2.0 * math.pi / NZ)
    cos = (np.cos(angle) / math.sqrt(NZ)).astype(ml_dtypes.bfloat16)
    sin = (np.sin(angle) / math.sqrt(NZ)).astype(ml_dtypes.bfloat16)
    cz = cos.reshape(NZ, 64, 16).transpose(2, 0, 1)
    sz = sin.reshape(NZ, 64, 16).transpose(2, 0, 1)
    both = np.concatenate([cz, -sz], axis=2)
    z_table = both.reshape(CHIPS, 2, NZ, LANES).transpose(0, 2, 1, 3).reshape(CHIPS, NZ, 2 * LANES)
    y_table = np.stack([cos, sin])
    return np.ascontiguousarray(z_table), np.ascontiguousarray(y_table)


def pack_kernel(counts, anchors, helpers, home, positions, forces, out):
    bins = lax.broadcasted_iota(jnp.int32, (BINS_DEV, BIN), 0)
    slot = lax.broadcasted_iota(jnp.int32, (BINS_DEV, BIN), 1)
    limit = jnp.zeros((BINS_DEV, BIN), jnp.int32)
    for b in range(BINS_DEV):
        limit = jnp.where(bins == b, counts[b], limit)
    live = jnp.where(slot < limit, forces[...], 0.0)
    largest = jnp.max(jnp.abs(live), axis=1, keepdims=True)
    power = jnp.clip(jnp.ceil(jnp.log(largest) * (1.0 / math.log(2.0))), -126.0, 1.0)
    scaled = live * jnp.exp2(-power) * TOP
    code = jnp.clip(jnp.floor(scaled + 0.5), -TOP, TOP).astype(jnp.int32)
    exponent = power.astype(jnp.int32)
    lane = lax.broadcasted_iota(jnp.int32, (1, LANES), 1)
    meta = jnp.zeros((1, LANES), jnp.int32)
    for b in range(BINS_DEV):
        place = jnp.clip((positions[b] - LOW) * (1.0 / STEP) + 0.5, 0.0, 65535.0).astype(jnp.int32)
        first = place[0:1] | (place[1:2] << 16)
        second = place[2:3] | (code[b : b + 1] << 16)
        out[4 * b : 4 * b + 1, :] = first[:, :LANES]
        out[4 * b + 1 : 4 * b + 2, :] = first[:, LANES:]
        out[4 * b + 2 : 4 * b + 3, :] = second[:, :LANES]
        out[4 * b + 3 : 4 * b + 4, :] = second[:, LANES:]
        meta = jnp.where(lane == b, counts[b], meta)
        meta = jnp.where(lane == 16 + b, home[0] * (NY // 16) + anchors[1, b], meta)
        meta = jnp.where(lane == 32 + b, anchors[0, b], meta)
        meta = jnp.where(lane == 48 + b, anchors[2, b], meta)
        meta = jnp.where(lane == 64 + b, helpers[b], meta)
        meta = jnp.where(lane == 80 + b, exponent[b : b + 1, 0:1], meta)
    out[META:ROWS, :] = jnp.broadcast_to(meta, (ROWS - META, LANES))


def pack(positions, forces, counts, anchors, helpers, home):
    smem = pl.BlockSpec(memory_space=pltpu.SMEM)
    vmem = pl.BlockSpec(memory_space=pltpu.VMEM)
    return pl.pallas_call(
        pack_kernel,
        out_shape=jax.ShapeDtypeStruct((ROWS, LANES), jnp.int32),
        in_specs=[smem, smem, smem, smem, vmem, vmem],
        out_specs=vmem,
        name="pack",
    )(counts, anchors, helpers, home, positions, forces)


def gather_bins(metas, slab, lists, group):
    rows, offsets, ys, zs, powers = lists
    total = jnp.int32(0)
    for s, meta in enumerate(metas):

        def source(src, total, meta=meta, s=s):
            def more(state):
                b, _ = state
                return jnp.logical_and(b < BINS_DEV, meta[src, jnp.minimum(b, BINS_DEV - 1)] > 0)

            def add(state):
                b, k = state
                rows[k] = (s * CHIPS + src) * ROWS + 4 * b
                offsets[k] = XS * (slab + s) - meta[src, 32 + b]
                ys[k] = meta[src, 16 + b]
                zs[k] = meta[src, 48 + b]
                powers[k] = meta[src, 80 + b]
                return b + 1, k + 1

            return lax.while_loop(more, add, (jnp.int32(0), total))[1]

        total = lax.fori_loop(0, CHIPS, source, total)
    for extra in range(group):
        rows[total + extra] = 0
        offsets[total + extra] = 0
        ys[total + extra] = 0
        zs[total + extra] = 0
        powers[total + extra] = -1000
    return total


def add_bins(total, lists, group, data, wave, grid):
    rows, offsets, ys, zs, powers = lists
    plane = lax.broadcasted_iota(jnp.int32, (XS, LANES), 0)
    cell = lax.broadcasted_iota(jnp.int32, (PATCH, LANES), 0).astype(jnp.float32) * WIDTH

    def one(k):
        row = rows[k]
        index = plane + offsets[k]
        inside = jnp.logical_and(index >= 0, index < PATCH)
        along_x = index.astype(jnp.float32) * WIDTH
        scale = jnp.exp2(jnp.full((1, LANES), powers[k], jnp.int32).astype(jnp.float32)) * (1.0 / TOP)
        left, right = [], []
        for half in range(2):
            first = data[pl.ds(row + half, 1), :]
            second = data[pl.ds(row + 2 + half, 1), :]
            px = (first & 0xFFFF).astype(jnp.float32) * (STEP * WIDTH) + LOW * WIDTH
            py = ((first >> 16) & 0xFFFF).astype(jnp.float32) * (STEP * WIDTH) + LOW * WIDTH
            pz = (second & 0xFFFF).astype(jnp.float32) * (STEP * WIDTH) + LOW * WIDTH
            force = (second >> 16).astype(jnp.float32) * scale
            dx, dy, dz = along_x - px, cell - py, cell - pz
            ax = jnp.where(inside, jnp.exp2(-(dx * dx)) * force, 0.0)
            ay = jnp.exp2(-(dy * dy))
            az = jnp.exp2(-(dz * dz))
            products = [ay * ax[x : x + 1, :] for x in range(XS)]
            left.append(jnp.concatenate(products, axis=0).astype(jnp.bfloat16))
            right.append(az.astype(jnp.bfloat16))
        patch = lax.dot_general(
            jnp.concatenate(left, axis=1),
            jnp.concatenate(right, axis=1),
            (((1,), (1,)), ((), ())),
            preferred_element_type=jnp.float32,
        ).astype(jnp.bfloat16)
        turn = jnp.concatenate([wave[c, pl.ds(zs[k], PATCH), :] for c in range(2)], axis=1)
        return jnp.dot(patch, turn.astype(jnp.bfloat16), preferred_element_type=jnp.float32)

    def several(i, carry):
        found = [one(group * i + u) for u in range(group)]
        for u in range(group):
            y = ys[group * i + u]
            for c in range(2):
                for x in range(XS):
                    at = pl.ds((c * XS + x) * DEPTH + y, PATCH)
                    grid[at, :] += found[u][x * PATCH : (x + 1) * PATCH, c * LANES : (c + 1) * LANES]
        return carry

    lax.fori_loop(0, (total + group - 1) // group, several, 0)

def near_kernel(chip, meta, block, table, grid, wave, load, *lists):
    def clear(i, carry):
        at = pl.ds(pl.multiple_of(i * DEPTH, XS), DEPTH)
        grid[at, :] = jnp.zeros((DEPTH, LANES), jnp.float32)
        return carry

    lax.fori_loop(0, 2 * XS, clear, 0)
    for c in range(2):
        lanes = slice(c * LANES, (c + 1) * LANES)
        wave[c, :NZ, :] = table[:, lanes].astype(jnp.float32)
        wave[c, NZ:, :] = table[:PATCH, lanes].astype(jnp.float32)
    lane = lax.broadcasted_iota(jnp.int32, (1, LANES), 1)
    count = jnp.zeros((1, LANES), jnp.int32)
    for src in range(CHIPS):
        row = block[src * ROWS + META : src * ROWS + META + 1, :]
        for b in range(BINS_DEV):
            count += jnp.where(lane == row[:, 64 + b : 65 + b], row[:, b : b + 1], 0)
    load[...] = jnp.broadcast_to(count, (8, LANES))
    total = gather_bins((meta,), 0, lists, NEAR)
    add_bins(total, lists, NEAR, block, wave, grid)


def far_kernel(core, m1, m2, m3, g1, g2, g3, wave, load, grid_in, other, grid, data, *lists):
    for s, block in enumerate((g1, g2, g3)):
        data[s * CHIPS * ROWS : (s + 1) * CHIPS * ROWS, :] = block[...]
    total = gather_bins((m1, m2, m3), 1, lists, FAR)
    add_bins(total, lists, FAR, data, wave, grid)
    theirs = 1 - core[0]

    def finish(i, carry):
        for c in range(2):
            start = pl.multiple_of((c * XS + i) * DEPTH, XS)
            grid[pl.ds(start, PATCH), :] += grid[pl.ds(start + NY, PATCH), :]
        start = pl.multiple_of((theirs * XS + i) * DEPTH, XS)
        other[pl.ds(pl.multiple_of(i * NY, NY), NY), :] = grid[pl.ds(start, NY), :].astype(jnp.bfloat16)
        return carry

    lax.fori_loop(0, XS, finish, 0)
    row = lax.broadcasted_iota(jnp.int32, (16, LANES), 0)
    count = jnp.concatenate([load[...], load[...]], axis=0)
    tail = jnp.where(row == 0, count >> 8, jnp.where(row == 1, count & 255, 0))
    other[XS * NY :, :] = tail.astype(jnp.float32).astype(jnp.bfloat16)


def bin_lists(slabs, group):
    return [pltpu.SMEM((slabs * CHIPS * BINS_DEV + group,), jnp.int32)] * 5


def spread_near(chip, meta, block, z_table):
    vmem = pl.BlockSpec(memory_space=pltpu.VMEM)
    return pl.pallas_call(
        near_kernel,
        out_shape=(
            pltpu.VMEM((2 * XS * DEPTH, LANES), jnp.float32),
            pltpu.VMEM((2, DEPTH, LANES), jnp.float32),
            pltpu.VMEM((8, LANES), jnp.int32),
        ),
        grid_spec=pltpu.PrefetchScalarGridSpec(
            num_scalar_prefetch=2,
            grid=(1,),
            in_specs=[vmem, pl.BlockSpec((None, NZ, 2 * LANES), lambda i, chip, meta: (chip[0], 0, 0))],
            out_specs=[vmem, vmem, vmem],
            scratch_shapes=bin_lists(1, NEAR),
        ),
        compiler_params=pltpu.CompilerParams(vmem_limit_bytes=24 * 2**20),
        cost_estimate=pl.CostEstimate(flops=2**32, bytes_accessed=2**23, transcendentals=2**20),
        name="near",
    )(chip, meta, block, z_table)


def spread_far(core, metas, blocks, wave, load, grid):
    smem = pl.BlockSpec(memory_space=pltpu.SMEM)
    vmem = pl.BlockSpec(memory_space=pltpu.VMEM)
    return pl.pallas_call(
        far_kernel,
        out_shape=(
            pltpu.VMEM((XS * NY + 16, LANES), jnp.bfloat16),
            pltpu.VMEM((2 * XS * DEPTH, LANES), jnp.float32),
        ),
        in_specs=[smem] * 4 + [vmem] * 6,
        out_specs=[vmem] * 2,
        input_output_aliases={9: 1},
        scratch_shapes=[pltpu.VMEM(((SLABS - 1) * CHIPS * ROWS, LANES), jnp.int32)] + bin_lists(SLABS - 1, FAR),
        compiler_params=pltpu.CompilerParams(vmem_limit_bytes=24 * 2**20),
        name="far",
    )(core, *metas, *blocks, wave, load, grid)


def rows_kernel(home, grid, other, load, table, out, helper_load):
    step = pl.program_id(0)

    @pl.when(step == 0)
    def _():
        theirs = other[XS * NY :, :].astype(jnp.float32)
        both = load[0:1, :].astype(jnp.float32) + theirs[0:1] * 256.0 + theirs[1:2]
        lane = lax.broadcasted_iota(jnp.int32, (1, LANES), 1)
        helper_load[0, 0] = jnp.sum(jnp.where(lane == home[0], both, 0.0)) * (1.0 / BIN)

    lines = []
    for x in range(PLANES):
        at = pl.ds(pl.multiple_of((step * PLANES + x) * NY, NY), NY)
        start = pl.multiple_of(((home[0] & 1) * XS + step * PLANES + x) * DEPTH, XS)
        both = grid[pl.ds(start, NY), :] + other[at, :].astype(jnp.float32)
        lines.append(both.astype(jnp.bfloat16).T)
    lines = jnp.concatenate(lines, axis=0)
    width = NY // TILES
    for t in range(TILES):
        at = slice(t * width, (t + 1) * width)
        cos = jnp.dot(lines, table[0, :, at], preferred_element_type=jnp.float32)
        sin = jnp.dot(lines, table[1, :, at], preferred_element_type=jnp.float32)
        for x in range(PLANES):
            real = slice(x * LANES, x * LANES + 64)
            imag = slice(x * LANES + 64, (x + 1) * LANES)
            out[0, x, :, at] = cos[real] + sin[imag]
            out[1, x, :, at] = cos[imag] - sin[real]


def along_rows(home, grid, other, load, y_table):
    smem = pl.BlockSpec(memory_space=pltpu.SMEM)
    vmem = pl.BlockSpec(memory_space=pltpu.VMEM)
    return pl.pallas_call(
        rows_kernel,
        out_shape=(
            jax.ShapeDtypeStruct((2, XS, 64, NY), jnp.float32),
            jax.ShapeDtypeStruct((1, 1), jnp.float32),
        ),
        grid=(XS // PLANES,),
        in_specs=[
            smem,
            vmem,
            vmem,
            vmem,
            vmem,
        ],
        out_specs=[pl.BlockSpec((2, PLANES, 64, NY), lambda i: (0, i, 0, 0)), smem],
        compiler_params=pltpu.CompilerParams(vmem_limit_bytes=24 * 2**20),
        name="rows",
    )(home, grid, other, load, y_table)


def slab_shift(block, distance):
    count = lax.axis_size("wide")
    return lax.ppermute(block, "wide", [(i, (i + distance) % count) for i in range(count)])


def chip_shift(block, distance):
    count = lax.axis_size("narrow")
    return lax.ppermute(block, "narrow", [(i, (i + 2 * distance) % count) for i in range(count)])


def partner(block):
    count = lax.axis_size("narrow")
    return lax.ppermute(block, "narrow", [(i, i ^ 1) for i in range(count)])


def ring(block):
    near = jnp.concatenate([chip_shift(block, 1), block, chip_shift(block, -1)], axis=0)
    before = chip_shift(near, 3)
    after = chip_shift(near[: 2 * ROWS], -3)
    return jnp.concatenate([near, before, after], axis=0)


def metas_of(block):
    return block.reshape(CHIPS, ROWS, LANES)[:, META]


def body(positions, forces, counts, anchors, helpers):
    z_table, y_table = tables()
    z_table = pltpu.with_memory_space_constraint(jnp.asarray(z_table), pltpu.HBM)
    y_table = pltpu.with_memory_space_constraint(jnp.asarray(y_table), pltpu.VMEM)
    index = lax.axis_index("narrow").astype(jnp.int32)
    home, chip, core = index.reshape(1), (index >> 1).reshape(1), (index & 1).reshape(1)
    packed = pack(positions, forces, counts, anchors, helpers.reshape(BINS_DEV), home)
    block = ring(packed)
    blocks = [slab_shift(block, d) for d in range(1, SLABS)]
    grid, wave, load = spread_near(chip, metas_of(block), block, z_table)
    other, grid = spread_far(core, [metas_of(g) for g in blocks], blocks, wave, load, grid)
    arrived = pltpu.with_memory_space_constraint(partner(other), pltpu.VMEM)
    spectrum, helper_load = along_rows(home, grid, arrived, load, y_table)
    return (spectrum, helper_load)


def solution(mesh):
    return jax.shard_map(
        body,
        mesh=mesh,
        in_specs=(
            P(("wide", "narrow"), None, None),
            P(("wide", "narrow"), None),
            P(("wide", "narrow")),
            P(None, ("wide", "narrow")),
            P(("wide", "narrow"), None),
        ),
        out_specs=(P(None, "wide", "narrow", None), P("wide", "narrow")),
        check_vma=False,
    )
```

```python
import functools
import math

import jax
import jax.numpy as jnp
import ml_dtypes
import numpy as np
from jax import lax
from jax.experimental import pallas as pl
from jax.experimental.pallas import tpu as pltpu
from jax.sharding import PartitionSpec as P

XS = 8
NY = 1024
NZ = 1024
PATCH = 24
BIN = 256
BINS_DEV = 12
SLABS = 4
CHIPS = 8
ROWS = 56
META = 4 * BINS_DEV
PARTICLES = CHIPS * META
RATE = 0.08
LOW = 6.0
STEP = 12.0 / 65535.0
TOP = 32767.0
TILES = 4
PLANES = 4
LANES = 128
NEAR = 16
FAR = 24
DEPTH = NY + PATCH
WIDTH = math.sqrt(RATE * math.log2(math.e))


@functools.lru_cache(maxsize=None)
def tables():
    ordinal = np.arange(NZ)
    phase = ordinal[:, None] * ordinal[None, :] % NZ
    angle = phase.astype(np.float64) * (2.0 * math.pi / NZ)
    cos = (np.cos(angle) / math.sqrt(NZ)).astype(ml_dtypes.bfloat16)
    sin = (np.sin(angle) / math.sqrt(NZ)).astype(ml_dtypes.bfloat16)
    cz = cos.reshape(NZ, 64, 16).transpose(2, 0, 1)
    sz = sin.reshape(NZ, 64, 16).transpose(2, 0, 1)
    both = np.concatenate([cz, -sz], axis=2)
    z_table = both.reshape(CHIPS, 2, NZ, LANES).transpose(0, 2, 1, 3).reshape(CHIPS, NZ, 2 * LANES)
    y_table = np.stack([cos, sin])
    return np.ascontiguousarray(z_table), np.ascontiguousarray(y_table)


def pack_kernel(counts, anchors, helpers, home, positions, forces, out):
    bins = lax.broadcasted_iota(jnp.int32, (BINS_DEV, BIN), 0)
    slot = lax.broadcasted_iota(jnp.int32, (BINS_DEV, BIN), 1)
    limit = jnp.zeros((BINS_DEV, BIN), jnp.int32)
    for b in range(BINS_DEV):
        limit = jnp.where(bins == b, counts[b], limit)
    live = jnp.where(slot < limit, forces[...], 0.0)
    largest = jnp.max(jnp.abs(live), axis=1, keepdims=True)
    power = jnp.clip(jnp.ceil(jnp.log(largest) * (1.0 / math.log(2.0))), -126.0, 1.0)
    scaled = live * jnp.exp2(-power) * TOP
    code = jnp.clip(jnp.floor(scaled + 0.5), -TOP, TOP).astype(jnp.int32)
    exponent = power.astype(jnp.int32)
    lane = lax.broadcasted_iota(jnp.int32, (1, LANES), 1)
    meta = jnp.zeros((1, LANES), jnp.int32)
    for b in range(BINS_DEV):
        place = jnp.clip((positions[b] - LOW) * (1.0 / STEP) + 0.5, 0.0, 65535.0).astype(jnp.int32)
        first = place[0:1] | (place[1:2] << 16)
        second = place[2:3] | (code[b : b + 1] << 16)
        out[4 * b : 4 * b + 1, :] = first[:, :LANES]
        out[4 * b + 1 : 4 * b + 2, :] = first[:, LANES:]
        out[4 * b + 2 : 4 * b + 3, :] = second[:, :LANES]
        out[4 * b + 3 : 4 * b + 4, :] = second[:, LANES:]
        meta = jnp.where(lane == b, counts[b], meta)
        meta = jnp.where(lane == 16 + b, home[0] * (NY // 16) + anchors[1, b], meta)
        meta = jnp.where(lane == 32 + b, anchors[0, b], meta)
        meta = jnp.where(lane == 48 + b, anchors[2, b], meta)
        meta = jnp.where(lane == 64 + b, helpers[b], meta)
        meta = jnp.where(lane == 80 + b, exponent[b : b + 1, 0:1], meta)
    out[META:ROWS, :] = jnp.broadcast_to(meta, (ROWS - META, LANES))


def pack(positions, forces, counts, anchors, helpers, home):
    smem = pl.BlockSpec(memory_space=pltpu.SMEM)
    vmem = pl.BlockSpec(memory_space=pltpu.VMEM)
    return pl.pallas_call(
        pack_kernel,
        out_shape=jax.ShapeDtypeStruct((ROWS, LANES), jnp.int32),
        in_specs=[smem, smem, smem, smem, vmem, vmem],
        out_specs=vmem,
        name="pack",
    )(counts, anchors, helpers, home, positions, forces)


def gather_bins(metas, slab, lists, group):
    rows, offsets, ys, zs, powers = lists
    total = jnp.int32(0)
    for s, meta in enumerate(metas):

        def source(src, total, meta=meta, s=s):
            def more(state):
                b, _ = state
                return jnp.logical_and(b < BINS_DEV, meta[src, jnp.minimum(b, BINS_DEV - 1)] > 0)

            def add(state):
                b, k = state
                rows[k] = (s * CHIPS + src) * META + 4 * b
                offsets[k] = XS * (slab + s) - meta[src, 32 + b]
                ys[k] = meta[src, 16 + b]
                zs[k] = meta[src, 48 + b]
                powers[k] = meta[src, 80 + b]
                return b + 1, k + 1

            return lax.while_loop(more, add, (jnp.int32(0), total))[1]

        total = lax.fori_loop(0, CHIPS, source, total)
    for extra in range(group):
        rows[total + extra] = 0
        offsets[total + extra] = 0
        ys[total + extra] = 0
        zs[total + extra] = 0
        powers[total + extra] = -1000
    return total


def add_bins(total, lists, group, data, wave, grid):
    rows, offsets, ys, zs, powers = lists
    plane = lax.broadcasted_iota(jnp.int32, (XS, LANES), 0)
    cell = lax.broadcasted_iota(jnp.int32, (PATCH, LANES), 0).astype(jnp.float32) * WIDTH

    def one(k):
        row = rows[k]
        index = plane + offsets[k]
        inside = jnp.logical_and(index >= 0, index < PATCH)
        along_x = index.astype(jnp.float32) * WIDTH
        scale = jnp.exp2(jnp.full((1, LANES), powers[k], jnp.int32).astype(jnp.float32)) * (1.0 / TOP)
        left, right = [], []
        for half in range(2):
            first = data[pl.ds(row + half, 1), :]
            second = data[pl.ds(row + 2 + half, 1), :]
            px = (first & 0xFFFF).astype(jnp.float32) * (STEP * WIDTH) + LOW * WIDTH
            py = ((first >> 16) & 0xFFFF).astype(jnp.float32) * (STEP * WIDTH) + LOW * WIDTH
            pz = (second & 0xFFFF).astype(jnp.float32) * (STEP * WIDTH) + LOW * WIDTH
            force = (second >> 16).astype(jnp.float32) * scale
            dx, dy, dz = along_x - px, cell - py, cell - pz
            ax = jnp.where(inside, jnp.exp2(-(dx * dx)) * force, 0.0)
            ay = jnp.exp2(-(dy * dy))
            az = jnp.exp2(-(dz * dz))
            products = [ay * ax[x : x + 1, :] for x in range(XS)]
            left.append(jnp.concatenate(products, axis=0).astype(jnp.bfloat16))
            right.append(az.astype(jnp.bfloat16))
        patch = lax.dot_general(
            jnp.concatenate(left, axis=1),
            jnp.concatenate(right, axis=1),
            (((1,), (1,)), ((), ())),
            preferred_element_type=jnp.float32,
        ).astype(jnp.bfloat16)
        turn = jnp.concatenate([wave[c, pl.ds(zs[k], PATCH), :] for c in range(2)], axis=1)
        return jnp.dot(patch, turn.astype(jnp.bfloat16), preferred_element_type=jnp.float32)

    def several(i, carry):
        found = [one(group * i + u) for u in range(group)]
        for u in range(group):
            y = ys[group * i + u]
            for c in range(2):
                for x in range(XS):
                    at = pl.ds((c * XS + x) * DEPTH + y, PATCH)
                    grid[at, :] += found[u][x * PATCH : (x + 1) * PATCH, c * LANES : (c + 1) * LANES]
        return carry

    lax.fori_loop(0, (total + group - 1) // group, several, 0)

def near_kernel(chip, meta, block, table, grid, wave, load, *lists):
    def clear(i, carry):
        at = pl.ds(pl.multiple_of(i * DEPTH, XS), DEPTH)
        grid[at, :] = jnp.zeros((DEPTH, LANES), jnp.float32)
        return carry

    lax.fori_loop(0, 2 * XS, clear, 0)
    for c in range(2):
        lanes = slice(c * LANES, (c + 1) * LANES)
        wave[c, :NZ, :] = table[:, lanes].astype(jnp.float32)
        wave[c, NZ:, :] = table[:PATCH, lanes].astype(jnp.float32)
    lane = lax.broadcasted_iota(jnp.int32, (1, LANES), 1)
    count = jnp.zeros((1, LANES), jnp.int32)
    for src in range(CHIPS):
        row = block[PARTICLES + src : PARTICLES + src + 1, :]
        for b in range(BINS_DEV):
            count += jnp.where(lane == row[:, 64 + b : 65 + b], row[:, b : b + 1], 0)
    load[...] = jnp.broadcast_to(count, (8, LANES))
    total = gather_bins((meta,), 0, lists, NEAR)
    add_bins(total, lists, NEAR, block, wave, grid)


def far_kernel(core, m1, m2, m3, g1, g2, g3, wave, load, grid_in, other, grid, data, *lists):
    for s, block in enumerate((g1, g2, g3)):
        data[s * PARTICLES : (s + 1) * PARTICLES, :] = block[:PARTICLES, :]
    total = gather_bins((m1, m2, m3), 1, lists, FAR)
    add_bins(total, lists, FAR, data, wave, grid)
    theirs = 1 - core[0]

    def finish(i, carry):
        for c in range(2):
            start = pl.multiple_of((c * XS + i) * DEPTH, XS)
            grid[pl.ds(start, PATCH), :] += grid[pl.ds(start + NY, PATCH), :]
        start = pl.multiple_of((theirs * XS + i) * DEPTH, XS)
        other[pl.ds(pl.multiple_of(i * NY, NY), NY), :] = grid[pl.ds(start, NY), :].astype(jnp.bfloat16)
        return carry

    lax.fori_loop(0, XS, finish, 0)
    row = lax.broadcasted_iota(jnp.int32, (16, LANES), 0)
    count = jnp.concatenate([load[...], load[...]], axis=0)
    tail = jnp.where(row == 0, count >> 8, jnp.where(row == 1, count & 255, 0))
    other[XS * NY :, :] = tail.astype(jnp.float32).astype(jnp.bfloat16)


def bin_lists(slabs, group):
    return [pltpu.SMEM((slabs * CHIPS * BINS_DEV + group,), jnp.int32)] * 5


def spread_near(chip, meta, block, z_table):
    vmem = pl.BlockSpec(memory_space=pltpu.VMEM)
    return pl.pallas_call(
        near_kernel,
        out_shape=(
            pltpu.VMEM((2 * XS * DEPTH, LANES), jnp.float32),
            pltpu.VMEM((2, DEPTH, LANES), jnp.float32),
            pltpu.VMEM((8, LANES), jnp.int32),
        ),
        grid_spec=pltpu.PrefetchScalarGridSpec(
            num_scalar_prefetch=2,
            grid=(1,),
            in_specs=[vmem, pl.BlockSpec((None, NZ, 2 * LANES), lambda i, chip, meta: (chip[0], 0, 0))],
            out_specs=[vmem, vmem, vmem],
            scratch_shapes=bin_lists(1, NEAR),
        ),
        compiler_params=pltpu.CompilerParams(vmem_limit_bytes=24 * 2**20),
        cost_estimate=pl.CostEstimate(flops=2**32, bytes_accessed=2**23, transcendentals=2**20),
        name="near",
    )(chip, meta, block, z_table)


def spread_far(core, metas, blocks, wave, load, grid):
    smem = pl.BlockSpec(memory_space=pltpu.SMEM)
    vmem = pl.BlockSpec(memory_space=pltpu.VMEM)
    return pl.pallas_call(
        far_kernel,
        out_shape=(
            pltpu.VMEM((XS * NY + 16, LANES), jnp.bfloat16),
            pltpu.VMEM((2 * XS * DEPTH, LANES), jnp.float32),
        ),
        in_specs=[smem] * 4 + [vmem] * 6,
        out_specs=[vmem] * 2,
        input_output_aliases={9: 1},
        scratch_shapes=[pltpu.VMEM(((SLABS - 1) * PARTICLES, LANES), jnp.int32)] + bin_lists(SLABS - 1, FAR),
        compiler_params=pltpu.CompilerParams(vmem_limit_bytes=24 * 2**20),
        name="far",
    )(core, *metas, *blocks, wave, load, grid)


def rows_kernel(home, grid, other, load, table, out, helper_load):
    step = pl.program_id(0)

    @pl.when(step == 0)
    def _():
        theirs = other[XS * NY :, :].astype(jnp.float32)
        both = load[0:1, :].astype(jnp.float32) + theirs[0:1] * 256.0 + theirs[1:2]
        lane = lax.broadcasted_iota(jnp.int32, (1, LANES), 1)
        helper_load[0, 0] = jnp.sum(jnp.where(lane == home[0], both, 0.0)) * (1.0 / BIN)

    lines = []
    for x in range(PLANES):
        at = pl.ds(pl.multiple_of((step * PLANES + x) * NY, NY), NY)
        start = pl.multiple_of(((home[0] & 1) * XS + step * PLANES + x) * DEPTH, XS)
        both = grid[pl.ds(start, NY), :] + other[at, :].astype(jnp.float32)
        lines.append(both.astype(jnp.bfloat16).T)
    lines = jnp.concatenate(lines, axis=0)
    width = NY // TILES
    for t in range(TILES):
        at = slice(t * width, (t + 1) * width)
        cos = jnp.dot(lines, table[0, :, at], preferred_element_type=jnp.float32)
        sin = jnp.dot(lines, table[1, :, at], preferred_element_type=jnp.float32)
        for x in range(PLANES):
            real = slice(x * LANES, x * LANES + 64)
            imag = slice(x * LANES + 64, (x + 1) * LANES)
            out[0, x, :, at] = cos[real] + sin[imag]
            out[1, x, :, at] = cos[imag] - sin[real]


def along_rows(home, grid, other, load, y_table):
    smem = pl.BlockSpec(memory_space=pltpu.SMEM)
    vmem = pl.BlockSpec(memory_space=pltpu.VMEM)
    return pl.pallas_call(
        rows_kernel,
        out_shape=(
            jax.ShapeDtypeStruct((2, XS, 64, NY), jnp.float32),
            jax.ShapeDtypeStruct((1, 1), jnp.float32),
        ),
        grid=(XS // PLANES,),
        in_specs=[
            smem,
            vmem,
            vmem,
            vmem,
            vmem,
        ],
        out_specs=[pl.BlockSpec((2, PLANES, 64, NY), lambda i: (0, i, 0, 0)), smem],
        compiler_params=pltpu.CompilerParams(vmem_limit_bytes=24 * 2**20),
        name="rows",
    )(home, grid, other, load, y_table)


def slab_shift(block, distance):
    count = lax.axis_size("wide")
    return lax.ppermute(block, "wide", [(i, (i + distance) % count) for i in range(count)])


def chip_shift(block, distance):
    count = lax.axis_size("narrow")
    return lax.ppermute(block, "narrow", [(i, (i + 2 * distance) % count) for i in range(count)])


def partner(block):
    count = lax.axis_size("narrow")
    return lax.ppermute(block, "narrow", [(i, i ^ 1) for i in range(count)])


def merge_kernel(near, before, after, out, meta):
    src = 0
    for piece in (near, before, after):
        for at in range(0, piece.shape[0], ROWS):
            out[src * META : (src + 1) * META, :] = piece[at : at + META, :]
            out[PARTICLES + src : PARTICLES + src + 1, :] = piece[at + META : at + META + 1, :]
            meta[src : src + 1, :] = piece[at + META : at + META + 1, :]
            src += 1


def merge(pieces):
    vmem = pl.BlockSpec(memory_space=pltpu.VMEM)
    return pl.pallas_call(
        merge_kernel,
        out_shape=(
            pltpu.VMEM((PARTICLES + CHIPS, LANES), jnp.int32),
            pltpu.VMEM((CHIPS, LANES), jnp.int32),
        ),
        in_specs=[vmem] * 3,
        out_specs=[vmem] * 2,
        name="merge",
    )(*[pltpu.with_memory_space_constraint(piece, pltpu.VMEM) for piece in pieces])


def ring(block):
    near = jnp.concatenate([chip_shift(block, 1), block, chip_shift(block, -1)], axis=0)
    before = chip_shift(near, 3)
    after = chip_shift(near[: 2 * ROWS], -3)
    return merge((near, before, after))


def metas_of(block):
    return block[PARTICLES:]


def body(positions, forces, counts, anchors, helpers):
    z_table, y_table = tables()
    z_table = pltpu.with_memory_space_constraint(jnp.asarray(z_table), pltpu.HBM)
    y_table = pltpu.with_memory_space_constraint(jnp.asarray(y_table), pltpu.VMEM)
    index = lax.axis_index("narrow").astype(jnp.int32)
    home, chip, core = index.reshape(1), (index >> 1).reshape(1), (index & 1).reshape(1)
    packed = pack(positions, forces, counts, anchors, helpers.reshape(BINS_DEV), home)
    block, meta = ring(packed)
    blocks = [slab_shift(block, d) for d in range(1, SLABS)]
    grid, wave, load = spread_near(chip, meta, block, z_table)
    other, grid = spread_far(core, [metas_of(g) for g in blocks], blocks, wave, load, grid)
    arrived = pltpu.with_memory_space_constraint(partner(other), pltpu.VMEM)
    spectrum, helper_load = along_rows(home, grid, arrived, load, y_table)
    return (spectrum, helper_load)


def solution(mesh):
    return jax.shard_map(
        body,
        mesh=mesh,
        in_specs=(
            P(("wide", "narrow"), None, None),
            P(("wide", "narrow"), None),
            P(("wide", "narrow")),
            P(None, ("wide", "narrow")),
            P(("wide", "narrow"), None),
        ),
        out_specs=(P(None, "wide", "narrow", None), P("wide", "narrow")),
        check_vma=False,
    )
```
